32 devices in a mesh: space: 8 (over z, x), ray: 4 (over y, core).
Axes of the slice: x: 2, y: 2, z: 4, core: 2. Of those that a mesh axis runs over, the one named last changes fastest.
Arguments:
- excite: float32 [2, 16384], P(None, ('space', 'ray')), may hold values from -6 to 6
- history: float32 [64, 16384], P(None, ('space', 'ray')), may hold values from -6 to 6
- near_mats: float32 [128, 8, 3, 128, 128], P(('space', 'ray')), may hold values from -0.109375 to 0.109375
- neighbours: int32 [128, 8], P(('space', 'ray')), may hold values from 0 to 127, as said below
- self_inverse: float32 [128, 128, 128], P(('space', 'ray')), may hold values from -3 to 4
- radiation: float32 [128, 8192, 128], P(('space', 'ray')), may hold values from -0.1875 to 0.1875
- directions: float32 [3, 8192], replicated, may hold values from -1 to 1, as said below
- centers: float32 [3, 8], replicated, may hold values from -1 to 16, as said below
- counts: int32 [128], P(('space', 'ray')), may hold values from 32 to 128
Outputs:
- currents: float32 [2, 16384], P(None, ('space', 'ray'))
The draws below stay inside these ranges and needn't reach their ends.
Inputs may be any that keep to these rules, and one draw needn't show every extreme that they name: `neighbours`: every neighbour is a box within 4 boxes of its row's box. `directions`: each column is a unit vector. `centers`: the first coordinate of column c lies within 0.4 of 2 c, the others within -1 and 1.
All inputs are finite; a program needn't handle non-finite values.
Results may differ from the reference program's by a relative error of at most 0.0003.
Values sent between devices are 32-bit elements; how exact they have to be, the bound alone decides.
A program may use at most 128 MiB of HBM per device.

```python
import jax
import jax.numpy as jnp
from jax import lax

PB = 128
BOX_DEV = 4
K = 64
TAU = 48
KN = 3
NB = 8
RAYS = 8192
STEPS = 2
BOXES = 128
PATCHES = 16384
CLUSTERS = 8


def draw_neighbours(key, part):
    box_ids = jnp.arange(BOXES, dtype=jnp.int32)[:, None]
    offsets = jax.random.randint(jax.random.fold_in(key, 11), (BOXES, NB), -BOX_DEV, BOX_DEV + 1, dtype=jnp.int32)
    return jnp.clip(box_ids + offsets, 0, BOXES - 1).astype(jnp.int32)


def draw_self_inverse(key, part):
    noise = jnp.clip(jax.random.normal(jax.random.fold_in(key, 12), (BOXES, PB, PB), jnp.float32), -6.0, 6.0)
    return jnp.eye(PB, dtype=jnp.float32)[None] + 0.5 * noise / jnp.sqrt(float(PB))


def draw_directions(key, part):
    raw = jax.random.normal(jax.random.fold_in(key, 13), (3, RAYS), jnp.float32)
    length = jnp.sqrt(jnp.sum(raw * raw, axis=0, keepdims=True)) + 1e-06
    return raw / length


def draw_centers(key, part):
    first = 2.0 * jnp.arange(CLUSTERS, dtype=jnp.float32) + jax.random.uniform(jax.random.fold_in(key, 14), (CLUSTERS,), jnp.float32, -0.4, 0.4)
    others = jax.random.uniform(jax.random.fold_in(key, 15), (2, CLUSTERS), jnp.float32, -1.0, 1.0)
    return jnp.concatenate([first[None], others], axis=0)


def touch_ends(drawn, rng, smallest, top_value):
    place = [jax.random.randint(jax.random.fold_in(rng, axis), (), 0, length) for axis, length in enumerate(drawn.shape)]
    longest = drawn.shape.index(max(drawn.shape))
    neighbour = place[:longest] + [(place[longest] + 1) % drawn.shape[longest]] + place[longest + 1:]
    return drawn.at[tuple(place)].set(smallest).at[tuple(neighbour)].set(top_value)


def level_of(key, dims, shards, smallest, high):
    gain = 1.0
    for dim, shards_of in shards:
        draws = jax.random.uniform(jax.random.fold_in(jax.random.fold_in(key, 6), dim), (shards_of,), jnp.float32, smallest / len(shards), high / len(shards))
        gain = gain * jnp.repeat(jnp.exp(draws), dims[dim] // shards_of).reshape((-1,) + (1,) * (len(dims) - 1 - dim))
    return gain


def scatter_about(rng, extent, spread, limit, shards=(), kind=jnp.bfloat16):
    result = spread * jax.random.normal(rng, extent, jnp.float32)
    if shards:
        result = result * level_of(rng, extent, shards, -0.22, 0.18)
    return jnp.clip(result, -limit, limit).astype(kind)


def setup_inputs(seed: int = 0) -> dict:
    key_list = jax.random.split(jax.random.key(seed), 10)
    excite = scatter_about(key_list[0], (STEPS, PATCHES), 1.0, 6.0, ((1, 32),), jnp.float32)
    history = scatter_about(key_list[1], (K, PATCHES), 1.0, 6.0, ((1, 32),), jnp.float32)
    near_mats = scatter_about(key_list[2], (BOXES, NB, KN, PB, PB), (PB * NB * KN) ** -0.5, 0.109375, ((0, 32),), jnp.float32)
    neighbours = draw_neighbours(jax.random.fold_in(key_list[9], 71), 0)
    self_inverse = draw_self_inverse(jax.random.fold_in(key_list[9], 71), 0)
    radiation = scatter_about(key_list[5], (BOXES, RAYS, PB), (PB * RAYS // 1024) ** -0.5, 0.1875, ((0, 32),), jnp.float32)
    directions = draw_directions(jax.random.fold_in(key_list[9], 71), 0)
    centers = draw_centers(jax.random.fold_in(key_list[9], 71), 0)
    counts = touch_ends(jax.random.randint(key_list[8], (BOXES,), PB // 4, PB + 1), jax.random.fold_in(key_list[8], 1), PB // 4, PB).astype(jnp.int32)
    return dict(excite=excite, history=history, near_mats=near_mats, neighbours=neighbours, self_inverse=self_inverse, radiation=radiation, directions=directions, centers=centers, counts=counts)


HIGHEST_PRECISION = lax.Precision.HIGHEST

def temporal_basis(levels, length, lag_steps):
    orders = jnp.arange(levels, dtype=jnp.float32)
    return jnp.sqrt(2.0 / length) * jnp.cos(jnp.pi * (orders[:, None] + 0.5) * (lag_steps[None, :] + 0.5) / length)

def pair_lags(unit_dirs, source_centre, target_centre, length, reach):
    separation = target_centre[:, None, :] - source_centre[:, :, None]
    along = jnp.einsum('xd,xab->dab', unit_dirs, separation, precision=HIGHEST_PRECISION)
    return length * 0.125 + length * 0.375 * (1.0 + along / reach)

def pair_gains(unit_dirs, source_centre, target_centre, source_ids, target_ids):
    separation = target_centre[:, None, :] - source_centre[:, :, None]
    distant = jnp.abs(target_ids[None, :] - source_ids[:, None]) >= 2
    distance = jnp.sqrt(lax.optimization_barrier(jnp.sum(separation * separation, axis=0)))
    distance = jnp.where(distant, distance, 1.0)
    cosine = jnp.einsum('xd,xab->dab', unit_dirs, separation, precision=HIGHEST_PRECISION) / distance[None]
    return jnp.where(distant[None], (1.0 + cosine) / (2.0 * distance[None]), 0.0)

def reference(excite, history, near_mats, neighbours, self_inverse, radiation, directions, centers, counts):
    box_total = near_mats.shape[0]
    per_cluster = box_total // CLUSTERS
    reach = 2.0 * CLUSTERS + 4.0
    basis = temporal_basis(TAU, K, jnp.arange(K, dtype=jnp.float32))
    cluster_ids = jnp.arange(CLUSTERS, dtype=jnp.int32)
    radiation_map = radiation.reshape(CLUSTERS, per_cluster, RAYS, PB)
    occupied = jnp.arange(PB, dtype=jnp.int32)[None, :] < counts[:, None]
    results = []
    for instant in range(STEPS):
        recent = history[:KN].reshape(KN, box_total, PB)
        nearby = recent[:, neighbours]
        near_term = jnp.einsum('bjkpq,kbjq->bp', near_mats, nearby, precision=HIGHEST_PRECISION)
        projected = jnp.dot(basis, history, precision=HIGHEST_PRECISION).reshape(TAU, CLUSTERS, per_cluster, PB)
        outgoing = jnp.einsum('cbdp,mcbp->cdm', radiation_map, projected, precision=HIGHEST_PRECISION)
        flipped = jnp.transpose(outgoing, (2, 1, 0))

        def target_sample(target):
            target_centre = lax.dynamic_slice_in_dim(centers, target, 1, 1)
            target_ids = jnp.reshape(target, (1,)).astype(jnp.int32)
            weights = pair_gains(directions, centers, target_centre, cluster_ids, target_ids)[:, :, 0]
            lags = pair_lags(directions, centers, target_centre, K, reach)[:, :, 0]
            evaluate = temporal_basis(TAU, K, lags.reshape(-1)).reshape(TAU, RAYS, CLUSTERS)
            per_pair = lax.optimization_barrier(jnp.sum(flipped * evaluate, axis=0))
            return lax.optimization_barrier(jnp.sum(weights * per_pair, axis=1))
        sampled = lax.map(target_sample, cluster_ids)
        far_term = jnp.einsum('cbdp,cd->cbp', radiation_map, sampled, precision=HIGHEST_PRECISION).reshape(box_total, PB)
        right_side = excite[instant].reshape(box_total, PB) - near_term - far_term
        solved = jnp.einsum('bpq,bq->bp', self_inverse, right_side, precision=HIGHEST_PRECISION)
        solved = jnp.where(occupied, solved, 0.0).reshape(box_total * PB)
        results.append(solved)
        history = jnp.concatenate([solved[None], history[:-1]], axis=0)
    return jnp.stack(results)
```

```python
import functools
import math

import jax
import jax.numpy as jnp
import numpy as np
from jax import lax
from jax.experimental import pallas as pl
from jax.experimental.pallas import tpu as pltpu
from jax.sharding import PartitionSpec as P

TAU = 48
KN = 3
BLOCK = 512
MESH = pl.DeviceIdType.MESH
EXACT = lax.Precision.HIGHEST
F32 = jnp.float32
BF16 = jnp.bfloat16


def dot_nt(a, b, precision=None):
    return lax.dot_general(a, b, (((1,), (1,)), ((), ())), precision=precision, preferred_element_type=F32)


def split(x):
    hi = x.astype(BF16)
    return hi, (x - hi.astype(F32)).astype(BF16)


def stacked(x):
    hi, lo = split(x)
    return jnp.concatenate([hi, lo], axis=0)


def clenshaw(row, twice, shape):
    later, latest = jnp.zeros(shape, F32), jnp.zeros(shape, F32)
    for m in reversed(range(TAU)):
        later, latest = row(m) + twice * later - latest, later
    return later - latest


def kernel(
    ns, nr, first_column,
    excite, history, basis, directions, centers, counts, neighbours, near_hbm, inv_hbm, rad_hbm,
    out,
    rad, rh, rl, near, inv, window, cwindow, twice, weight, ochunk, y1, y2, e0, p2, got1, send2, got2, samp,
    near1, near2, cur,
    rad_sem, near_sem, inv_sem, win_s, win_r, s1, r1, s2, r2, s3, r3,
):
    boxes, pb = near_hbm.shape[0], near_hbm.shape[-1]
    slots = near_hbm.shape[1]
    length = history.shape[0]
    rq = rad.shape[2]
    db = ochunk.shape[1]
    c, r = lax.axis_index("space"), lax.axis_index("ray")
    lin = c * nr + r
    total = ns * nr
    norm = math.sqrt(2.0 / length)

    def place(b, j):
        return jnp.clip(neighbours[b, j] - lin * boxes + boxes, 0, 3 * boxes - 1)

    def quarter(i):
        return (r + 1 + i) % nr

    loads = []
    for i in range(nr):
        start = pl.multiple_of(quarter(i) * rq, rq)
        load = pltpu.make_async_copy(rad_hbm.at[:, pl.ds(start, rq), :], rad.at[i], rad_sem.at[i])
        load.start()
        loads.append(load)
    near_load = pltpu.make_async_copy(near_hbm, near, near_sem)
    near_load.start()
    inv_load = pltpu.make_async_copy(inv_hbm, inv, inv_sem)
    inv_load.start()

    right, left = (lin + 1) % total, (lin + total - 1) % total
    right_id, left_id = (right // nr, right % nr), (left // nr, left % nr)
    barrier = pltpu.get_barrier_semaphore()
    peers = [(c, (r + o) % nr) for o in range(1, nr)] + [((c + o) % ns, r) for o in range(1, ns)]
    peers += [right_id, left_id]
    for peer in peers:
        pl.semaphore_signal(barrier, inc=1, device_id=peer, device_id_type=MESH)

    row_ids = lax.broadcasted_iota(jnp.int32, (ns, 128), 0)
    seps = []
    for x in range(3):
        column = jnp.zeros((ns, 128), F32)
        for s in range(ns):
            column = jnp.where(row_ids == s, centers[x, s], column)
        seps.append(column - centers[x, c])
    distant = jnp.abs(row_ids - c) >= 2
    distance = jnp.sqrt(seps[0] * seps[0] + seps[1] * seps[1] + seps[2] * seps[2])
    distance = jnp.where(distant, distance, 1.0)
    half_gain = jnp.where(distant, 0.5 / distance, 0.0)
    reach = 2.0 * ns + 4.0
    for i in range(nr):

        @pl.loop(0, rq // db)
        def _(j, i=i):
            here = pl.ds(pl.multiple_of(j * db, db), db)
            there = pl.ds(pl.multiple_of(quarter(i) * rq + j * db, db), db)
            along = jnp.zeros((ns, db), F32)
            for x in range(3):
                along = along + directions[x : x + 1, there] * seps[x][:, :1]
            half = (math.pi * (0.5 * length + 0.5) / length + along * (math.pi * 0.375 / reach)) * 0.5
            ch = jnp.cos(half)
            twice[i, :, here] = 4.0 * ch * ch - 2.0
            weight[i, :, here] = half_gain[:, :1] * (1.0 + along / distance[:, :1]) * (ch * norm)

    x1 = stacked(jnp.dot(basis[...], history[...], precision=EXACT, preferred_element_type=F32))
    for b in range(boxes):
        window[boxes + b] = history[0:8, b * pb : (b + 1) * pb]

    pl.semaphore_wait(barrier, len(peers))
    sent = []

    def send(src, dst, ssem, rsem, target):
        copy = pltpu.make_async_remote_copy(
            src_ref=src, dst_ref=dst, send_sem=ssem, recv_sem=rsem, device_id=target, device_id_type=MESH
        )
        copy.start()
        sent.append(copy)
        return copy

    def exchange(ref, t):
        mine = ref.at[pl.ds(boxes, boxes)]
        return [
            send(mine, ref.at[pl.ds(0, boxes)], win_s.at[t, 0], win_r.at[t, 0], right_id),
            send(mine, ref.at[pl.ds(2 * boxes, boxes)], win_s.at[t, 1], win_r.at[t, 1], left_id),
        ]

    def scatter(src, t, i):
        return send(src.at[i], got1.at[t, i], s1.at[t, i], r1.at[t, i], (c, quarter(i)))

    def translate(src, t, copies):
        for copy in copies:
            copy.wait_recv()
        reduced = src[nr - 1]
        for i in range(nr - 1):
            reduced = reduced + got1[t, i]
        for s in range(ns):
            send2[t, s] = reduced[s : s + 1, :]
        return [
            send(send2.at[t, (c + o) % ns], got2.at[t, o - 1], s2.at[t, o - 1], r2.at[t, o - 1], ((c + o) % ns, r))
            for o in range(1, ns)
        ]

    def collect(t, copies):
        for copy in copies:
            copy.wait_recv()
        value = got2[t, 0]
        for o in range(1, ns - 1):
            value = value + got2[t, o]
        samp[t, nr - 1] = value
        return [
            send(samp.at[t, nr - 1], samp.at[t, nr - 1 - o], s3.at[t, o - 1], r3.at[t, o - 1], (c, (r + o) % nr))
            for o in range(1, nr)
        ]

    def far_part(t, i):
        s = stacked(jnp.broadcast_to(samp[t, i], (8, rq)))
        top = jnp.dot(s, rh[i], preferred_element_type=F32)
        low = jnp.dot(s[:8], rl[i], preferred_element_type=F32)
        return top[:8] + top[8:] + low

    def solve(t, copies, near_ref):
        far = far_part(t, nr - 1)
        for copy in copies:
            copy.wait_recv()
        for i in range(nr - 1):
            far = far + far_part(t, i)
        lanes = lax.broadcasted_iota(jnp.int32, (8, pb), 1)
        for b in range(boxes):
            cols = slice(b * pb, (b + 1) * pb)
            rhs = excite[t : t + 1, cols] - near_ref[b] - far[:, cols]
            value = jnp.where(lanes < counts[b], dot_nt(rhs, inv[b], EXACT), 0.0)
            cur[b] = value
            out[t : t + 1, cols] = value[:1]

    win_copies = exchange(window, 0)

    copies = []
    for i in range(nr):
        loads[i].wait()

        @pl.loop(0, rq // db)
        def _(j, i=i):
            here = pl.ds(pl.multiple_of(j * db, db), db)
            x = jnp.concatenate([rad[i, b, here, :] for b in range(boxes)], axis=1)
            hi, lo = split(x)
            rh[i, here, :] = hi
            rl[i, here, :] = lo
            both = dot_nt(x1, hi)
            value = both[: 2 * TAU] + both[2 * TAU :] + dot_nt(x1[: 2 * TAU], lo)
            ochunk[...] = value[:TAU]
            p2[i, :, here] = value[TAU:]
            y1[i, :, here] = weight[i, :, here] * clenshaw(
                lambda m: ochunk[m : m + 1, :], twice[i, :, here], (ns, db)
            )

        if i < nr - 1:
            copies.append(scatter(y1, 0, i))

    def later_part(i):
        @pl.loop(0, rq // db)
        def _(j):
            here = pl.ds(pl.multiple_of(j * db, db), db)
            w, c2 = weight[i, :, here], twice[i, :, here]
            y2[i, :, here] = w * clenshaw(lambda m: p2[i, m : m + 1, here], c2, (ns, db))
            e0[i, :, here] = w * clenshaw(lambda m: first_column[m], c2, (ns, db))

    def near_part():
        near_load.wait()
        for copy in win_copies:
            copy.wait_recv()
        ones = jnp.ones((8, pb), F32)

        @pl.loop(0, boxes)
        def _(b):
            now, later = jnp.zeros((pb, pb), F32), jnp.zeros((pb, pb), F32)
            for j in range(slots):
                rows = window[place(b, j)]
                for k in range(KN):
                    mat = near[b, j, k]
                    now = now + mat * rows[k : k + 1]
                    if k:
                        later = later + mat * rows[k - 1 : k]
            near1[b] = dot_nt(ones, now, EXACT)
            near2[b] = dot_nt(ones, later, EXACT)

    near_part()
    copies = translate(y1, 0, copies)
    for i in range(nr // 2):
        later_part(i)
    copies = collect(0, copies)
    for i in range(nr // 2, nr):
        later_part(i)
    inv_load.wait()
    solve(0, copies, near1)

    for b in range(boxes):
        cwindow[boxes + b] = cur[b]
    win_copies = exchange(cwindow, 1)
    xc = stacked(jnp.concatenate([cur[b] for b in range(boxes)], axis=1))
    copies = []
    for i in range(nr):

        @pl.loop(0, rq // db)
        def _(j, i=i):
            here = pl.ds(pl.multiple_of(j * db, db), db)
            top = dot_nt(xc, rh[i, here, :])
            low = dot_nt(xc[:8], rl[i, here, :])
            value = (top[:8] + top[8:] + low)[:1]
            y2[i, :, here] = y2[i, :, here] + e0[i, :, here] * value

        if i < nr - 1:
            copies.append(scatter(y2, 1, i))
    for copy in win_copies:
        copy.wait_recv()
    ones = jnp.ones((8, pb), F32)

    @pl.loop(0, boxes)
    def _(b):
        now = jnp.zeros((pb, pb), F32)
        for j in range(slots):
            now = now + near[b, j, 0] * cwindow[place(b, j)][:1]
        near2[b] = near2[b] + dot_nt(ones, now, EXACT)

    copies = translate(y2, 1, copies)
    copies = collect(1, copies)
    solve(1, copies, near2)
    for copy in sent:
        copy.wait_send()


def local(ns, nr, excite, history, near_mats, neighbours, self_inverse, radiation, directions, centers, counts):
    boxes, rays, pb = radiation.shape
    length = history.shape[0]
    steps = excite.shape[0]
    rq = rays // nr
    db = min(BLOCK, rq)
    patches = boxes * pb
    orders, times = np.arange(TAU)[:, None] + 0.5, np.arange(length)[None, :] + 0.5
    basis = np.sqrt(2.0 / length) * np.cos(np.pi * orders * times / length)
    shifted = np.concatenate([basis[:, 1:], np.zeros((TAU, 1))], axis=1)
    first_column = [float(v) for v in basis[:, 0]]
    both = jnp.asarray(np.concatenate([basis, shifted], axis=0), F32)
    vmem = pl.BlockSpec(memory_space=pltpu.VMEM)
    smem = pl.BlockSpec(memory_space=pltpu.SMEM)
    hbm = pl.BlockSpec(memory_space=pl.ANY)
    dma = pltpu.SemaphoreType.DMA
    return pl.pallas_call(
        functools.partial(kernel, ns, nr, first_column),
        out_shape=jax.ShapeDtypeStruct((steps, patches), F32),
        in_specs=[vmem] * 4 + [smem] * 3 + [hbm] * 3,
        out_specs=vmem,
        scratch_shapes=[
            pltpu.VMEM((nr, boxes, rq, pb), F32),
            pltpu.VMEM((nr, rq, patches), BF16),
            pltpu.VMEM((nr, rq, patches), BF16),
            pltpu.VMEM(near_mats.shape, F32),
            pltpu.VMEM(self_inverse.shape, F32),
            pltpu.VMEM((3 * boxes, 8, pb), F32),
            pltpu.VMEM((3 * boxes, 8, pb), F32),
            pltpu.VMEM((nr, ns, rq), F32),
            pltpu.VMEM((nr, ns, rq), F32),
            pltpu.VMEM((TAU, db), F32),
            pltpu.VMEM((nr, ns, rq), F32),
            pltpu.VMEM((nr, ns, rq), F32),
            pltpu.VMEM((nr, ns, rq), F32),
            pltpu.VMEM((nr, TAU, rq), F32),
            pltpu.VMEM((steps, nr - 1, ns, rq), F32),
            pltpu.VMEM((steps, ns, 1, rq), F32),
            pltpu.VMEM((steps, ns - 1, 1, rq), F32),
            pltpu.VMEM((steps, nr, 1, rq), F32),
            pltpu.VMEM((boxes, 8, pb), F32),
            pltpu.VMEM((boxes, 8, pb), F32),
            pltpu.VMEM((boxes, 8, pb), F32),
            dma((nr,)), dma(()), dma(()),
            dma((steps, 2)), dma((steps, 2)),
            dma((steps, nr - 1)), dma((steps, nr - 1)),
            dma((steps, ns - 1)), dma((steps, ns - 1)),
            dma((steps, nr - 1)), dma((steps, nr - 1)),
        ],
        compiler_params=pltpu.CompilerParams(
            collective_id=0, has_side_effects=True, vmem_limit_bytes=58 * 1024 * 1024
        ),
    )(excite, history, both, directions, centers, counts, neighbours, near_mats, self_inverse, radiation)


def solution(mesh):
    placed = (
        P(None, ("space", "ray")),
        P(None, ("space", "ray")),
        P(("space", "ray"), None, None, None, None),
        P(("space", "ray"), None),
        P(("space", "ray"), None, None),
        P(("space", "ray"), None, None),
        P(),
        P(),
        P(("space", "ray")),
    )
    return jax.shard_map(
        functools.partial(local, mesh.shape["space"], mesh.shape["ray"]),
        mesh=mesh,
        in_specs=placed,
        out_specs=P(None, ("space", "ray")),
        check_vma=False,
    )
```

```python
import functools
import math

import jax
import jax.numpy as jnp
import numpy as np
from jax import lax
from jax.experimental import pallas as pl
from jax.experimental.pallas import tpu as pltpu
from jax.sharding import PartitionSpec as P

TAU = 48
KN = 3
BLOCK = 512
MESH = pl.DeviceIdType.MESH
EXACT = lax.Precision.HIGHEST
F32 = jnp.float32
BF16 = jnp.bfloat16


def dot_nt(a, b, precision=None):
    return lax.dot_general(a, b, (((1,), (1,)), ((), ())), precision=precision, preferred_element_type=F32)


def split(x):
    hi = x.astype(BF16)
    return hi, (x - hi.astype(F32)).astype(BF16)


def stacked(x):
    hi, lo = split(x)
    return jnp.concatenate([hi, lo], axis=0)


def clenshaw(row, twice, shape):
    later, latest = jnp.zeros(shape, F32), jnp.zeros(shape, F32)
    for m in reversed(range(TAU)):
        later, latest = row(m) + twice * later - latest, later
    return later - latest


def kernel(
    ns, nr, first_column,
    excite, history, basis, directions, centers, counts, neighbours, near_hbm, inv_hbm, rad_hbm,
    out,
    rad, rh, rl, near, inv, window, cwindow, twice, weight, ochunk, y1, y2, e0, p2, got1, send2, got2, samp,
    near1, near2, cur, wl, gotw,
    rad_sem, near_sem, inv_sem, win_s, win_r, s1, r1, s2, r2, s3, r3, sw, rw,
):
    boxes, pb = near_hbm.shape[0], near_hbm.shape[-1]
    slots = near_hbm.shape[1]
    length = history.shape[0]
    rq = rad.shape[2]
    db = ochunk.shape[1]
    c, r = lax.axis_index("space"), lax.axis_index("ray")
    lin = c * nr + r
    total = ns * nr
    norm = math.sqrt(2.0 / length)

    def place(b, j):
        return jnp.clip(neighbours[b, j] - lin * boxes + boxes, 0, 3 * boxes - 1)

    def quarter(i):
        return (r + 1 + i) % nr

    loads = []
    for i in range(nr):
        start = pl.multiple_of(quarter(i) * rq, rq)
        load = pltpu.make_async_copy(rad_hbm.at[:, pl.ds(start, rq), :], rad.at[i], rad_sem.at[i])
        load.start()
        loads.append(load)
    near_load = pltpu.make_async_copy(near_hbm, near, near_sem)
    near_load.start()
    inv_load = pltpu.make_async_copy(inv_hbm, inv, inv_sem)
    inv_load.start()

    right, left = (lin + 1) % total, (lin + total - 1) % total
    right_id, left_id = (right // nr, right % nr), (left // nr, left % nr)
    barrier = pltpu.get_barrier_semaphore()
    peers = [(c, (r + o) % nr) for o in range(1, nr)] + [((c + o) % ns, r) for o in range(1, ns)]
    peers += [right_id, left_id]
    for peer in peers:
        pl.semaphore_signal(barrier, inc=1, device_id=peer, device_id_type=MESH)

    row_ids = lax.broadcasted_iota(jnp.int32, (ns, 128), 0)
    seps = []
    for x in range(3):
        column = jnp.zeros((ns, 128), F32)
        for s in range(ns):
            column = jnp.where(row_ids == s, centers[x, s], column)
        seps.append(column - centers[x, c])
    distant = jnp.abs(row_ids - c) >= 2
    distance = jnp.sqrt(seps[0] * seps[0] + seps[1] * seps[1] + seps[2] * seps[2])
    distance = jnp.where(distant, distance, 1.0)
    half_gain = jnp.where(distant, 0.5 / distance, 0.0)
    reach = 2.0 * ns + 4.0
    for i in range(nr):

        @pl.loop(0, rq // db)
        def _(j, i=i):
            here = pl.ds(pl.multiple_of(j * db, db), db)
            there = pl.ds(pl.multiple_of(quarter(i) * rq + j * db, db), db)
            along = jnp.zeros((ns, db), F32)
            for x in range(3):
                along = along + directions[x : x + 1, there] * seps[x][:, :1]
            half = (math.pi * (0.5 * length + 0.5) / length + along * (math.pi * 0.375 / reach)) * 0.5
            ch = jnp.cos(half)
            twice[i, :, here] = 4.0 * ch * ch - 2.0
            weight[i, :, here] = half_gain[:, :1] * (1.0 + along / distance[:, :1]) * (ch * norm)

    x1 = stacked(jnp.dot(basis[...], history[...], precision=EXACT, preferred_element_type=F32))
    for b in range(boxes):
        window[boxes + b] = history[0:8, b * pb : (b + 1) * pb]

    pl.semaphore_wait(barrier, len(peers))
    sent = []

    def send(src, dst, ssem, rsem, target):
        copy = pltpu.make_async_remote_copy(
            src_ref=src, dst_ref=dst, send_sem=ssem, recv_sem=rsem, device_id=target, device_id_type=MESH
        )
        copy.start()
        sent.append(copy)
        return copy

    def exchange(ref, t):
        mine = ref.at[pl.ds(boxes, boxes)]
        return [
            send(mine, ref.at[pl.ds(0, boxes)], win_s.at[t, 0], win_r.at[t, 0], right_id),
            send(mine, ref.at[pl.ds(2 * boxes, boxes)], win_s.at[t, 1], win_r.at[t, 1], left_id),
        ]

    def scatter(src, t, i):
        return send(src.at[i], got1.at[t, i], s1.at[t, i], r1.at[t, i], (c, quarter(i)))

    def reduce(src, t, copies):
        for copy in copies:
            copy.wait_recv()
        reduced = src[nr - 1]
        for i in range(nr - 1):
            reduced = reduced + got1[t, i]
        return reduced

    def translate(reduced, t):
        for s in range(ns):
            send2[t, s] = reduced[s : s + 1, :]
        return [
            send(send2.at[t, (c + o) % ns], got2.at[t, o - 1], s2.at[t, o - 1], r2.at[t, o - 1], ((c + o) % ns, r))
            for o in range(1, ns)
        ]

    def collect(t, copies):
        for copy in copies:
            copy.wait_recv()
        value = got2[t, 0]
        for o in range(1, ns - 1):
            value = value + got2[t, o]
        samp[t, nr - 1] = value
        return [
            send(samp.at[t, nr - 1], samp.at[t, nr - 1 - o], s3.at[t, o - 1], r3.at[t, o - 1], (c, (r + o) % nr))
            for o in range(1, nr)
        ]

    def far_part(t, i):
        s = stacked(jnp.broadcast_to(samp[t, i], (8, rq)))
        top = jnp.dot(s, rh[i], preferred_element_type=F32)
        low = jnp.dot(s[:8], rl[i], preferred_element_type=F32)
        return top[:8] + top[8:] + low

    def solve(t, copies, near_ref):
        far = far_part(t, nr - 1)
        for copy in copies:
            copy.wait_recv()
        for i in range(nr - 1):
            far = far + far_part(t, i)
        lanes = lax.broadcasted_iota(jnp.int32, (8, pb), 1)
        for b in range(boxes):
            cols = slice(b * pb, (b + 1) * pb)
            rhs = excite[t : t + 1, cols] - near_ref[b] - far[:, cols]
            value = jnp.where(lanes < counts[b], dot_nt(rhs, inv[b], EXACT), 0.0)
            cur[b] = value
            out[t : t + 1, cols] = value[:1]

    win_copies = exchange(window, 0)

    copies = []
    for i in range(nr):
        loads[i].wait()

        @pl.loop(0, rq // db)
        def _(j, i=i):
            here = pl.ds(pl.multiple_of(j * db, db), db)
            x = jnp.concatenate([rad[i, b, here, :] for b in range(boxes)], axis=1)
            hi, lo = split(x)
            rh[i, here, :] = hi
            rl[i, here, :] = lo
            both = dot_nt(x1, hi)
            value = both[: 2 * TAU] + both[2 * TAU :] + dot_nt(x1[: 2 * TAU], lo)
            ochunk[...] = value[:TAU]
            p2[i, :, here] = value[TAU:]
            y1[i, :, here] = weight[i, :, here] * clenshaw(
                lambda m: ochunk[m : m + 1, :], twice[i, :, here], (ns, db)
            )

        if i < nr - 1:
            copies.append(scatter(y1, 0, i))

    def later_part(i):
        @pl.loop(0, rq // db)
        def _(j):
            here = pl.ds(pl.multiple_of(j * db, db), db)
            w, c2 = weight[i, :, here], twice[i, :, here]
            y2[i, :, here] = w * clenshaw(lambda m: p2[i, m : m + 1, here], c2, (ns, db))
            if i == nr - 1:
                e0[:, here] = w * clenshaw(lambda m: first_column[m], c2, (ns, db))

    def near_part():
        near_load.wait()
        for copy in win_copies:
            copy.wait_recv()
        ones = jnp.ones((8, pb), F32)

        @pl.loop(0, boxes)
        def _(b):
            now, later = jnp.zeros((pb, pb), F32), jnp.zeros((pb, pb), F32)
            for j in range(slots):
                rows = window[place(b, j)]
                for k in range(KN):
                    mat = near[b, j, k]
                    now = now + mat * rows[k : k + 1]
                    if k:
                        later = later + mat * rows[k - 1 : k]
            near1[b] = dot_nt(ones, now, EXACT)
            near2[b] = dot_nt(ones, later, EXACT)

    copies = translate(reduce(y1, 0, copies), 0)
    known = []
    for i in range(nr):
        later_part(i)
        if i < nr - 1:
            known.append(scatter(y2, 1, i))
    near_part()
    copies = collect(0, copies)
    inv_load.wait()
    solve(0, copies, near1)

    for b in range(boxes):
        cwindow[boxes + b] = cur[b]
    win_copies = exchange(cwindow, 1)
    xc = stacked(jnp.concatenate([cur[b] for b in range(boxes)], axis=1))
    copies = []
    for i in range(nr):

        @pl.loop(0, rq // db)
        def _(j, i=i):
            here = pl.ds(pl.multiple_of(j * db, db), db)
            top = dot_nt(xc, rh[i, here, :])
            low = dot_nt(xc[:8], rl[i, here, :])
            wl[i, :, here] = (top[:8] + top[8:] + low)[:1]

        if i < nr - 1:
            copies.append(send(wl.at[i], gotw.at[i], sw.at[i], rw.at[i], (c, quarter(i))))
    known = reduce(y2, 1, known)
    for copy in copies:
        copy.wait_recv()
    fresh = wl[nr - 1]
    for i in range(nr - 1):
        fresh = fresh + gotw[i]
    copies = translate(known + e0[...] * fresh, 1)
    for copy in win_copies:
        copy.wait_recv()
    ones = jnp.ones((8, pb), F32)

    @pl.loop(0, boxes)
    def _(b):
        now = jnp.zeros((pb, pb), F32)
        for j in range(slots):
            now = now + near[b, j, 0] * cwindow[place(b, j)][:1]
        near2[b] = near2[b] + dot_nt(ones, now, EXACT)

    copies = collect(1, copies)
    solve(1, copies, near2)
    for copy in sent:
        copy.wait_send()


def local(ns, nr, excite, history, near_mats, neighbours, self_inverse, radiation, directions, centers, counts):
    boxes, rays, pb = radiation.shape
    length = history.shape[0]
    steps = excite.shape[0]
    rq = rays // nr
    db = min(BLOCK, rq)
    patches = boxes * pb
    orders, times = np.arange(TAU)[:, None] + 0.5, np.arange(length)[None, :] + 0.5
    basis = np.sqrt(2.0 / length) * np.cos(np.pi * orders * times / length)
    shifted = np.concatenate([basis[:, 1:], np.zeros((TAU, 1))], axis=1)
    first_column = [float(v) for v in basis[:, 0]]
    both = jnp.asarray(np.concatenate([basis, shifted], axis=0), F32)
    vmem = pl.BlockSpec(memory_space=pltpu.VMEM)
    smem = pl.BlockSpec(memory_space=pltpu.SMEM)
    hbm = pl.BlockSpec(memory_space=pl.ANY)
    dma = pltpu.SemaphoreType.DMA
    return pl.pallas_call(
        functools.partial(kernel, ns, nr, first_column),
        out_shape=jax.ShapeDtypeStruct((steps, patches), F32),
        in_specs=[vmem] * 4 + [smem] * 3 + [hbm] * 3,
        out_specs=vmem,
        scratch_shapes=[
            pltpu.VMEM((nr, boxes, rq, pb), F32),
            pltpu.VMEM((nr, rq, patches), BF16),
            pltpu.VMEM((nr, rq, patches), BF16),
            pltpu.VMEM(near_mats.shape, F32),
            pltpu.VMEM(self_inverse.shape, F32),
            pltpu.VMEM((3 * boxes, 8, pb), F32),
            pltpu.VMEM((3 * boxes, 8, pb), F32),
            pltpu.VMEM((nr, ns, rq), F32),
            pltpu.VMEM((nr, ns, rq), F32),
            pltpu.VMEM((TAU, db), F32),
            pltpu.VMEM((nr, ns, rq), F32),
            pltpu.VMEM((nr, ns, rq), F32),
            pltpu.VMEM((ns, rq), F32),
            pltpu.VMEM((nr, TAU, rq), F32),
            pltpu.VMEM((steps, nr - 1, ns, rq), F32),
            pltpu.VMEM((steps, ns, 1, rq), F32),
            pltpu.VMEM((steps, ns - 1, 1, rq), F32),
            pltpu.VMEM((steps, nr, 1, rq), F32),
            pltpu.VMEM((boxes, 8, pb), F32),
            pltpu.VMEM((boxes, 8, pb), F32),
            pltpu.VMEM((boxes, 8, pb), F32),
            pltpu.VMEM((nr, 1, rq), F32),
            pltpu.VMEM((nr - 1, 1, rq), F32),
            dma((nr,)), dma(()), dma(()),
            dma((steps, 2)), dma((steps, 2)),
            dma((steps, nr - 1)), dma((steps, nr - 1)),
            dma((steps, ns - 1)), dma((steps, ns - 1)),
            dma((steps, nr - 1)), dma((steps, nr - 1)),
            dma((nr - 1,)), dma((nr - 1,)),
        ],
        compiler_params=pltpu.CompilerParams(
            collective_id=0, has_side_effects=True, vmem_limit_bytes=58 * 1024 * 1024
        ),
    )(excite, history, both, directions, centers, counts, neighbours, near_mats, self_inverse, radiation)


def solution(mesh):
    placed = (
        P(None, ("space", "ray")),
        P(None, ("space", "ray")),
        P(("space", "ray"), None, None, None, None),
        P(("space", "ray"), None),
        P(("space", "ray"), None, None),
        P(("space", "ray"), None, None),
        P(),
        P(),
        P(("space", "ray")),
    )
    return jax.shard_map(
        functools.partial(local, mesh.shape["space"], mesh.shape["ray"]),
        mesh=mesh,
        in_specs=placed,
        out_specs=P(None, ("space", "ray")),
        check_vma=False,
    )
```
